256 devices in a mesh: lat: 64 (over x, z, core), lev: 4 (over y).
Axes of the slice: x: 4, y: 4, z: 8, core: 2. Of those that a mesh axis runs over, the one named last changes fastest.
Arguments:
- fine_field: bfloat16 [2, 1280, 32, 1280], P(None, 'lat', 'lev'), may hold values from -6 to 6
- fwd_table: bfloat16 [320, 641, 1280], P('lat'), may hold values from -0.125 to 0.125
- inv_table: bfloat16 [320, 641, 640], P('lat'), may hold values from -0.25 to 0.25
- pair_order: int32 [320], replicated, may hold values from 0 to 319, each once
Outputs:
- coarse: bfloat16 [2, 640, 32, 1280], P(None, 'lat', 'lev')
The draws below stay inside these ranges and needn't reach their ends.
Inputs may be any that keep to these rules, and one draw needn't show every extreme that they name: Each value appears once; slot s holds the wavenumbers pair_order[s] and 639 - pair_order[s].
All inputs are finite; a program needn't handle non-finite values.
Results may differ from the reference program's by a relative error of at most 0.0059.
Values may be sent and summed in bfloat16 or wider, within the bound.
A program may use at most 128 MiB of HBM per device.

```python
import jax
import jax.numpy as jnp
from jax import lax

M = 640
NLATH = 1280
NCLATH = 640
LEV = 32
PAIRS = 320
DPAIR = 641


def block_levels(rng, extent, shards, least, top_value):
    level = 1.0
    for axis_at, parts in shards:
        steps = jax.random.uniform(jax.random.fold_in(jax.random.fold_in(rng, 6), axis_at), (parts,), jnp.float32, least / len(shards), top_value / len(shards))
        level = level * jnp.repeat(jnp.exp(steps), extent[axis_at] // parts).reshape((-1,) + (1,) * (len(extent) - 1 - axis_at))
    return level


def centred(rng, extent, scale, bound, shards=(), kind=jnp.bfloat16):
    drawn = jax.random.normal(rng, extent, jnp.float32) * scale
    if len(shards) > 0:
        drawn = block_levels(rng, extent, shards, -0.22, 0.18) * drawn
    return jnp.clip(drawn, min=-bound, max=bound).astype(kind)


def setup_inputs(seed: int = 0) -> dict:
    keys = jax.random.split(jax.random.key(seed), 5)
    return {
        "fine_field": centred(keys[0], (2, NLATH, LEV, 2 * M), 1.0, 6.0, ((1, 64), (2, 4))),
        "fwd_table": centred(keys[1], (PAIRS, DPAIR, NLATH), (2 * NLATH) ** -0.5, 0.125, ((0, 64),)),
        "inv_table": centred(keys[2], (PAIRS, DPAIR, NCLATH), M ** -0.5, 0.25, ((0, 64),)),
        "pair_order": jax.random.permutation(keys[3], PAIRS).astype(jnp.int32),
    }


def carried_mask(row_start, row_count, wave_ids):
    row_ids = row_start + jnp.arange(row_count, dtype=jnp.int32)
    return 2 * wave_ids[None, :] < 20 + 4 * row_ids[:, None]


def slot_groups(pair_ids, total_waves, table_rows):
    row_ids = jnp.arange(table_rows, dtype=jnp.int32)
    boundary = total_waves - pair_ids[:, None]
    second = row_ids[None, :] >= boundary
    offset = jnp.where(second, row_ids[None, :] - boundary, row_ids[None, :])
    return 2 * second.astype(jnp.int32) + offset % 2


def reference(fine_field, fwd_table, inv_table, pair_order):
    wave_ids = jnp.arange(M, dtype=jnp.int32)
    values = fine_field.astype(jnp.float32).reshape(2, NLATH, LEV, 2, M)
    keep_fine = carried_mask(0, NLATH, wave_ids)
    values = jnp.where(keep_fine[None, :, None, None, :], values, jnp.zeros((), jnp.float32))
    even_part = (values[0] + values[1]).astype(jnp.bfloat16)
    odd_part = (values[0] - values[1]).astype(jnp.bfloat16)
    folded = jnp.stack([even_part, odd_part])
    picked = jnp.stack([jnp.take(folded, pair_order, axis=4), jnp.take(folded, M - 1 - pair_order, axis=4)])
    per_slot = jnp.transpose(picked, (5, 0, 1, 3, 4, 2)).reshape(PAIRS, 4, LEV * 2, NLATH)
    groups = slot_groups(pair_order, M, M + 1)
    coarse_ids = jnp.arange(NCLATH, dtype=jnp.int32)

    def one_slot(bundle):
        slot_table, slot_data, slot_group, back_table, pair_id = bundle
        product = jnp.einsum("rl,gxl->rgx", slot_table.astype(jnp.float32), slot_data.astype(jnp.float32))
        spectra = jnp.take_along_axis(product, slot_group[:, None, None], axis=1)[:, 0, :].astype(jnp.bfloat16)
        chosen = slot_group[:, None] == jnp.arange(4, dtype=jnp.int32)[None, :]
        spread = jnp.where(chosen[:, :, None], spectra[:, None, :], jnp.zeros((), jnp.bfloat16))
        summed = jnp.einsum("rj,rgx->gxj", back_table.astype(jnp.float32), spread.astype(jnp.float32))
        summed = summed.reshape(2, 2, LEV, 2, NCLATH)
        halves = jnp.stack([summed[:, 0] + summed[:, 1], summed[:, 0] - summed[:, 1]], axis=1)
        pair_waves = jnp.stack([pair_id, M - 1 - pair_id])
        keep_coarse = 2 * pair_waves[:, None] < 20 + 4 * coarse_ids[None, :]
        kept = jnp.where(keep_coarse[:, None, None, None, :], halves, jnp.zeros((), jnp.float32))
        return kept.astype(jnp.bfloat16)

    results = lax.map(one_slot, (fwd_table, per_slot, groups, inv_table, pair_order))
    inverse_slots = jnp.zeros((PAIRS,), jnp.int32).at[pair_order].set(jnp.arange(PAIRS, dtype=jnp.int32))
    low_part = jnp.take(results[:, 0], inverse_slots, axis=0)
    high_part = jnp.take(results[:, 1], inverse_slots[::-1], axis=0)
    joined = jnp.concatenate([low_part, high_part], axis=0)
    return jnp.transpose(joined, (1, 4, 2, 3, 0)).reshape(2, NCLATH, LEV, 2 * M)
```

```python
import jax
import jax.numpy as jnp
from jax import lax
from jax.experimental import pallas as pl
from jax.experimental.pallas import tpu as pltpu
from jax.sharding import PartitionSpec as P

MESH = pl.DeviceIdType.MESH
WAVES = 640
FINE = 1280
COARSE = 640
BANDS = 64
BAND = FINE // BANDS
CBAND = COARSE // BANDS
SLOTS = 5
ROWS = 641
BF = jnp.bfloat16
F32 = jnp.float32


def lanes(shape):
    return lax.broadcasted_iota(jnp.int32, shape, len(shape) - 1)


def block_transpose(a):
    lane = lanes(a[0].shape)
    low = lane < 64
    even = (lane // 32) % 2 == 0
    c0 = jnp.where(low, a[0], pltpu.roll(a[2], 64, 1))
    c2 = jnp.where(low, pltpu.roll(a[0], 64, 1), a[2])
    c1 = jnp.where(low, a[1], pltpu.roll(a[3], 64, 1))
    c3 = jnp.where(low, pltpu.roll(a[1], 64, 1), a[3])
    b0 = jnp.where(even, c0, pltpu.roll(c1, 32, 1))
    b1 = jnp.where(even, pltpu.roll(c0, 96, 1), c1)
    b2 = jnp.where(even, c2, pltpu.roll(c3, 32, 1))
    b3 = jnp.where(even, pltpu.roll(c2, 96, 1), c3)
    return b0, b1, b2, b3


def half_swap(a, b):
    low = lanes(a.shape) < 64
    return (
        jnp.where(low, a, pltpu.roll(b, 64, 1)),
        jnp.where(low, pltpu.roll(a, 64, 1), b),
    )


def kernel(
    pair_ref, wave_ref, fine_ref, fwd_hbm, inv_hbm, out_ref,
    fwd, inv, folded, sel, wide, narrow, acc,
    send_ab, send_c, recv_ab, recv_c, back_ab, back_c, home_ab, home_c,
    fwd_sem, inv_sem, out_sem1, in_sem1, out_sem2, in_sem2,
):
    me = lax.axis_index("lat")
    lev = lax.axis_index("lev")
    barrier = pltpu.get_barrier_semaphore()

    @pl.loop(1, BANDS)
    def _(t):
        pl.semaphore_signal(
            barrier, inc=1, device_id=(lax.rem(me + t, BANDS), lev), device_id_type=MESH
        )

    for s in range(SLOTS):
        pltpu.make_async_copy(fwd_hbm.at[s], fwd.at[s], fwd_sem.at[s]).start()
        pltpu.make_async_copy(inv_hbm.at[s], inv.at[s], inv_sem.at[s]).start()

    @pl.loop(0, BAND)
    def _(i):
        north = fine_ref[0, i].astype(F32)
        south = fine_ref[1, i].astype(F32)
        m = lanes((8, 2 * WAVES))
        m = jnp.where(m >= WAVES, m - WAVES, m)
        kept = 2 * m < 20 + 4 * (me * BAND + i)
        even = jnp.where(kept, north + south, 0.0)
        odd = jnp.where(kept, north - south, 0.0)
        rows = jnp.concatenate(
            [even[:, :WAVES], even[:, WAVES:], odd[:, :WAVES], odd[:, WAVES:]], axis=0
        )
        folded[pl.ds(pl.multiple_of(i * 32, 32), 32), :] = rows.astype(BF)

    sel[...] = jnp.where(
        wave_ref[...] == lanes((WAVES, WAVES)), 1.0, 0.0
    ).astype(BF)

    def pick(first, count):
        return lax.dot_general(
            sel[first : first + count, :], folded[...], (((1,), (1,)), ((), ())),
            preferred_element_type=F32,
        )

    def exchange(src, dst, out_sem, in_sem):
        pltpu.make_async_copy(src.at[me], dst.at[me], in_sem).start()

        @pl.loop(1, BANDS)
        def _(t):
            to = lax.rem(me + t, BANDS)
            pltpu.make_async_remote_copy(
                src_ref=src.at[to], dst_ref=dst.at[me], send_sem=out_sem, recv_sem=in_sem,
                device_id=(to, lev), device_id_type=MESH,
            ).start()

    def arrive(dst, in_sem):
        pltpu.make_async_copy(dst, dst, in_sem).wait()

    def left(src, out_sem):
        part = src.at[pl.ds(0, BANDS - 1)]
        pltpu.make_async_copy(part, part, out_sem).wait()

    for ch in range(2):
        g = pick(256 * ch, 256)
        for q in range(BAND // 4):
            cols = g[:, 128 * q : 128 * (q + 1)]
            parts = block_transpose([cols[64 * k : 64 * (k + 1)] for k in range(4)])
            for k in range(4):
                wide[pl.ds(4 * q + k, BANDS, stride=BAND), :] = parts[k]
        send_ab.at[ch].reshape(FINE, 128)[...] = wide[...].astype(BF)
        if ch == 0:
            pl.semaphore_wait(barrier, BANDS - 1)
        exchange(send_ab.at[ch], recv_ab.at[ch], out_sem1.at[ch], in_sem1.at[ch])

    g = pick(512, 128)
    for q in range(BAND // 4):
        cols = g[:, 128 * q : 128 * (q + 1)]
        parts = half_swap(cols[:64], cols[64:])
        for k in range(2):
            wide[pl.ds(2 * q + k, BANDS, stride=BAND // 2), :] = parts[k]
    send_c.reshape(FINE // 2, 128)[...] = wide[: FINE // 2].astype(BF)
    exchange(send_c, recv_c, out_sem1.at[2], in_sem1.at[2])

    row = lax.broadcasted_iota(jnp.int32, (ROWS, 128), 0)
    lane = lanes((ROWS, 128))

    def transform(slot, x, fold_lanes, owned):
        pltpu.make_async_copy(fwd_hbm.at[slot], fwd.at[slot], fwd_sem.at[slot]).wait()
        product = jnp.dot(fwd[slot], x, preferred_element_type=F32)
        product = fold_lanes(product)
        boundary = WAVES - pair_ref[me * SLOTS + slot]
        second = row >= boundary
        parity = jnp.where(second, row - boundary, row) % 2
        wave = second.astype(jnp.int32)
        keep = owned(lane, wave) & ((lane // 16) % 2 == parity)
        spectra = jnp.where(keep, product, 0.0).astype(BF)
        pltpu.make_async_copy(inv_hbm.at[slot], inv.at[slot], inv_sem.at[slot]).wait()
        return lax.dot_general(
            inv[slot], spectra, (((0,), (0,)), ((), ())), preferred_element_type=F32
        )

    def hemispheres(v):
        first = (lanes(v.shape) // 16) % 2 == 0
        other = jnp.where(first, pltpu.roll(v, 112, 1), pltpu.roll(v, 16, 1))
        return other + jnp.where(first, v, -v)

    for ch in range(2):
        arrive(recv_ab.at[ch], in_sem1.at[ch])
        x = recv_ab.at[ch].reshape(FINE, 128)[...]
        v = 0.0
        for half in range(2):
            v += transform(
                2 * ch + half, x, lambda p: p,
                lambda lane, wave: lane // 32 == 2 * half + wave,
            )
        back_ab.at[ch].reshape(COARSE, 128)[...] = hemispheres(v).astype(BF)
        exchange(back_ab.at[ch], home_ab.at[ch], out_sem2.at[ch], in_sem2.at[ch])

    arrive(recv_c, in_sem1.at[2])
    x = recv_c.reshape(FINE // 2, 128)[...].astype(F32)
    upper = (lanes(x.shape) // 32) % 2 == 0
    wide[pl.ds(0, FINE // 2, stride=2), :] = jnp.where(upper, x, 0.0)
    wide[pl.ds(1, FINE // 2, stride=2), :] = jnp.where(upper, 0.0, x)
    v = transform(
        4, wide[...].astype(BF), lambda p: p + pltpu.roll(p, 96, 1),
        lambda lane, wave: lane // 32 == 2 * wave,
    )
    wide[:COARSE] = hemispheres(v)
    for k in range(CBAND // 2):
        a = wide[pl.ds(2 * k, BANDS, stride=CBAND), :]
        b = wide[pl.ds(2 * k + 1, BANDS, stride=CBAND), :]
        narrow[pl.ds(k, BANDS, stride=6), :] = jnp.where(
            (lanes(a.shape) // 32) % 2 == 0, a, pltpu.roll(b, 32, 1)
        )
    narrow[pl.ds(5, BANDS, stride=6), :] = jnp.zeros((BANDS, 128), F32)
    back_c.reshape(6 * BANDS, 128)[...] = narrow[...].astype(BF)
    exchange(back_c, home_c, out_sem2.at[2], in_sem2.at[2])

    def place(first, columns):
        count = columns.shape[0]
        return lax.dot_general(
            columns, sel[first : first + count, :], (((0,), (0,)), ((), ())),
            preferred_element_type=F32,
        )

    for ch in range(2):
        arrive(home_ab.at[ch], in_sem2.at[ch])
        wide[:COARSE] = home_ab.at[ch].reshape(COARSE, 128)[...].astype(F32)
        groups = []
        for q in range(3):
            js = [min(4 * q + k, CBAND - 1) for k in range(4)]
            groups.append(
                jnp.concatenate(
                    block_transpose([wide[pl.ds(j, BANDS, stride=CBAND), :] for j in js]), axis=0
                ).astype(BF)
            )
        placed = place(256 * ch, jnp.concatenate(groups, axis=1))
        if ch == 0:
            acc[...] = placed
        else:
            acc[...] += placed
    arrive(home_c, in_sem2.at[2])
    wide[: 6 * BANDS] = home_c.reshape(6 * BANDS, 128)[...].astype(F32)
    groups = []
    for q in range(3):
        parts = half_swap(*[wide[pl.ds(2 * q + k, BANDS, stride=6), :] for k in range(2)])
        groups.append(jnp.concatenate(parts, axis=0).astype(BF))
    acc[...] += place(512, jnp.concatenate(groups, axis=1))

    @pl.loop(0, CBAND)
    def _(j):
        rows = acc[pl.ds(pl.multiple_of(j * 32, 32), 32), :]
        kept = 2 * lanes(rows.shape) < 20 + 4 * (me * CBAND + j)
        rows = jnp.where(kept, rows, 0.0).astype(BF)
        for h in range(2):
            for c in range(2):
                at = 16 * h + 8 * c
                out_ref[h, j, :, c * WAVES : (c + 1) * WAVES] = rows[at : at + 8]

    for ch in range(2):
        left(send_ab.at[ch], out_sem1.at[ch])
        left(back_ab.at[ch], out_sem2.at[ch])
    left(send_c, out_sem1.at[2])
    left(back_c, out_sem2.at[2])


def on_device(fine_field, fwd_table, inv_table, pair_order):
    low = jnp.transpose(pair_order.reshape(BANDS, SLOTS))
    waves = jnp.stack([low, WAVES - 1 - low], axis=1).reshape(WAVES, 1)
    vmem = pl.BlockSpec(memory_space=pltpu.VMEM)
    hbm = pl.BlockSpec(memory_space=pl.ANY)
    ab1 = (2, BANDS, BAND // 2, 2, 128)
    c1 = (BANDS, BAND // 4, 2, 128)
    ab2 = (2, BANDS, CBAND // 2, 2, 128)
    c2 = (BANDS, 3, 2, 128)
    return pl.pallas_call(
        kernel,
        out_shape=jax.ShapeDtypeStruct((2, CBAND, 8, 2 * WAVES), BF),
        in_specs=[pl.BlockSpec(memory_space=pltpu.SMEM), vmem, vmem, hbm, hbm],
        out_specs=vmem,
        scratch_shapes=[
            pltpu.VMEM((SLOTS, ROWS, FINE), BF),
            pltpu.VMEM((SLOTS, ROWS, COARSE), BF),
            pltpu.VMEM((BAND * 32, WAVES), BF),
            pltpu.VMEM((WAVES, WAVES), BF),
            pltpu.VMEM((FINE, 128), F32),
            pltpu.VMEM((6 * BANDS, 128), F32),
            pltpu.VMEM((384, WAVES), F32),
            pltpu.VMEM(ab1, BF), pltpu.VMEM(c1, BF),
            pltpu.VMEM(ab1, BF), pltpu.VMEM(c1, BF),
            pltpu.VMEM(ab2, BF), pltpu.VMEM(c2, BF),
            pltpu.VMEM(ab2, BF), pltpu.VMEM(c2, BF),
            pltpu.SemaphoreType.DMA((SLOTS,)), pltpu.SemaphoreType.DMA((SLOTS,)),
            pltpu.SemaphoreType.DMA((3,)), pltpu.SemaphoreType.DMA((3,)),
            pltpu.SemaphoreType.DMA((3,)), pltpu.SemaphoreType.DMA((3,)),
        ],
        compiler_params=pltpu.CompilerParams(
            collective_id=0, has_side_effects=True, vmem_limit_bytes=48 << 20
        ),
    )(pair_order, waves, fine_field, fwd_table, inv_table)


def solution(mesh):
    return jax.shard_map(
        on_device,
        mesh=mesh,
        in_specs=(P(None, "lat", "lev", None), P("lat", None, None), P("lat", None, None), P()),
        out_specs=P(None, "lat", "lev", None),
        check_vma=False,
    )
```

```python
import jax
import jax.numpy as jnp
from jax import lax
from jax.experimental import pallas as pl
from jax.experimental.pallas import tpu as pltpu
from jax.sharding import PartitionSpec as P

MESH = pl.DeviceIdType.MESH
WAVES = 640
FINE = 1280
COARSE = 640
BANDS = 64
BAND = FINE // BANDS
CBAND = COARSE // BANDS
SLOTS = 5
PAIRS = BANDS * SLOTS
ROWS = 641
BF = jnp.bfloat16
F32 = jnp.float32


def lanes(shape):
    return lax.broadcasted_iota(jnp.int32, shape, len(shape) - 1)


def block_transpose(a):
    lane = lanes(a[0].shape)
    low = lane < 64
    even = (lane // 32) % 2 == 0
    c0 = jnp.where(low, a[0], pltpu.roll(a[2], 64, 1))
    c2 = jnp.where(low, pltpu.roll(a[0], 64, 1), a[2])
    c1 = jnp.where(low, a[1], pltpu.roll(a[3], 64, 1))
    c3 = jnp.where(low, pltpu.roll(a[1], 64, 1), a[3])
    b0 = jnp.where(even, c0, pltpu.roll(c1, 32, 1))
    b1 = jnp.where(even, pltpu.roll(c0, 96, 1), c1)
    b2 = jnp.where(even, c2, pltpu.roll(c3, 32, 1))
    b3 = jnp.where(even, pltpu.roll(c2, 96, 1), c3)
    return b0, b1, b2, b3


def half_swap(a, b):
    low = lanes(a.shape) < 64
    return (
        jnp.where(low, a, pltpu.roll(b, 64, 1)),
        jnp.where(low, pltpu.roll(a, 64, 1), b),
    )


def peer(me, u):
    ring = u // 8
    step = 4 + ((ring + 1) // 2) * (2 * (ring % 2) - 1)
    to = me + 16 * ((u % 8) // 2) + 2 * step + 1 - u % 2
    return lax.rem(to, BANDS)


def kernel(
    pair_hbm, fine_hbm, fwd_hbm, inv_hbm, out_ref,
    pair_ref, line, column, fine_ref, fwd, inv, folded, sel, turned, wide, narrow, acc,
    send_ab, send_c, recv_ab, recv_c, back_ab, back_c, home_ab, home_c,
    pair_sem, fine_sem, fwd_sem, inv_sem, out_sem1, in_sem1, out_sem2, in_sem2,
):
    me = lax.axis_index("lat")
    lev = lax.axis_index("lev")
    barrier = pltpu.get_barrier_semaphore()

    pieces = BAND // 4
    pair_copies = [
        pltpu.make_async_copy(pair_hbm, line, pair_sem.at[0]),
        pltpu.make_async_copy(pair_hbm, pair_ref, pair_sem.at[1]),
    ]
    fine_copies = [
        pltpu.make_async_copy(
            fine_hbm.at[:, pl.ds(4 * q, 4)], fine_ref.at[:, pl.ds(4 * q, 4)], fine_sem.at[q]
        )
        for q in range(pieces)
    ]
    for copy in pair_copies + fine_copies:
        copy.start()

    @pl.loop(1, BANDS, unroll=True)
    def _(t):
        pl.semaphore_signal(
            barrier, inc=1, device_id=(lax.rem(me + t, BANDS), lev), device_id_type=MESH
        )

    for s in range(SLOTS):
        pltpu.make_async_copy(fwd_hbm.at[s], fwd.at[s], fwd_sem.at[s]).start()
        pltpu.make_async_copy(inv_hbm.at[s], inv.at[s], inv_sem.at[s]).start()

    pair_copies[0].wait()
    column[...] = jnp.transpose(jnp.broadcast_to(line[...].reshape(1, PAIRS), (128, PAIRS)))
    for slot in range(SLOTS):
        low = column[pl.ds(slot, BANDS, stride=SLOTS), :]
        for k, wave in enumerate((low, WAVES - 1 - low)):
            at = (2 * slot + k) * BANDS
            for b in range(WAVES // 128):
                sel[at : at + BANDS, 128 * b : 128 * (b + 1)] = jnp.where(
                    wave == lanes(wave.shape) + 128 * b, 1.0, 0.0
                ).astype(BF)

    for at in (0, 256, 512):
        count = min(256, WAVES - at)
        turned[:, at : at + count] = jnp.transpose(sel[at : at + count, :])

    def fold(i):
        north = fine_ref[0, i].astype(F32)
        south = fine_ref[1, i].astype(F32)
        m = lanes((8, 2 * WAVES))
        m = jnp.where(m >= WAVES, m - WAVES, m)
        kept = 2 * m < 20 + 4 * (me * BAND + i)
        even = jnp.where(kept, north + south, 0.0)
        odd = jnp.where(kept, north - south, 0.0)
        rows = jnp.concatenate(
            [even[:, :WAVES], even[:, WAVES:], odd[:, :WAVES], odd[:, WAVES:]], axis=0
        )
        folded[32 * i : 32 * (i + 1), :] = rows.astype(BF)

    def facing(a, b, high):
        low = lanes(a.shape) < 64
        if high:
            return jnp.where(low, pltpu.roll(a, 64, 1), b)
        return jnp.where(low, a, pltpu.roll(b, 64, 1))

    def pick(first, count):
        g = jnp.dot(
            folded[...], turned[:, first : first + count], preferred_element_type=F32
        )
        return [g[32 * i : 32 * (i + 1)] for i in range(BAND)]

    def exchange(src, dst, out_sem, in_sem):
        pltpu.make_async_copy(src.at[me], dst.at[me], in_sem).start()

        @pl.loop(1, BANDS, unroll=9)
        def _(t):
            to = lax.rem(me + t, BANDS)
            pltpu.make_async_remote_copy(
                src_ref=src.at[to], dst_ref=dst.at[me], send_sem=out_sem, recv_sem=in_sem,
                device_id=(to, lev), device_id_type=MESH,
            ).start()

    def arrive(dst, in_sem):
        pltpu.make_async_copy(dst, dst, in_sem).wait()

    def left(src, out_sem):
        part = src.at[pl.ds(0, BANDS - 1)]
        pltpu.make_async_copy(part, part, out_sem).wait()

    for q in range(pieces):
        fine_copies[q].wait()
        for i in range(4 * q, 4 * (q + 1)):
            fold(i)
    for ch in range(2):
        g = pick(256 * ch, 256)
        for i in range(0, BAND, 2):
            blocks = []
            for k in range(4):
                at = 128 * (k // 2)
                a, b = g[i][:, at : at + 128], g[i + 1][:, at : at + 128]
                blocks.append(facing(a, b, k % 2 == 1))
            rows = jnp.transpose(jnp.concatenate(blocks, axis=0))
            for k in range(2):
                wide[pl.ds(i + k, BANDS, stride=BAND), :] = rows[64 * k : 64 * (k + 1)]
        send_ab.at[ch].reshape(FINE, 128)[...] = wide[...].astype(BF)
        if ch == 0:
            pl.semaphore_wait(barrier, BANDS - 1)
        exchange(send_ab.at[ch], recv_ab.at[ch], out_sem1.at[ch], in_sem1.at[ch])

    g = pick(512, 128)
    for i in range(0, BAND, 4):
        blocks = [facing(g[i + k % 2], g[i + 2 + k % 2], k >= 2) for k in range(4)]
        rows = jnp.transpose(jnp.concatenate(blocks, axis=0))
        for k in range(2):
            wide[pl.ds(i // 2 + k, BANDS, stride=BAND // 2), :] = rows[64 * k : 64 * (k + 1)]
    send_c.reshape(FINE // 2, 128)[...] = wide[: FINE // 2].astype(BF)
    exchange(send_c, recv_c, out_sem1.at[2], in_sem1.at[2])

    pair_copies[1].wait()
    row = lax.broadcasted_iota(jnp.int32, (ROWS, 128), 0)
    lane = lanes((ROWS, 128))

    def transform(slot, x, fold_lanes, owned):
        pltpu.make_async_copy(fwd_hbm.at[slot], fwd.at[slot], fwd_sem.at[slot]).wait()
        product = jnp.dot(fwd[slot], x, preferred_element_type=F32)
        product = fold_lanes(product)
        boundary = WAVES - pair_ref[me * SLOTS + slot]
        second = row >= boundary
        parity = jnp.where(second, row - boundary, row) % 2
        wave = second.astype(jnp.int32)
        keep = owned(lane, wave) & ((lane // 16) % 2 == parity)
        spectra = jnp.where(keep, product, 0.0).astype(BF)
        pltpu.make_async_copy(inv_hbm.at[slot], inv.at[slot], inv_sem.at[slot]).wait()
        return lax.dot_general(
            inv[slot], spectra, (((0,), (0,)), ((), ())), preferred_element_type=F32
        )

    def hemispheres(v):
        first = (lanes(v.shape) // 16) % 2 == 0
        other = jnp.where(first, pltpu.roll(v, 112, 1), pltpu.roll(v, 16, 1))
        return other + jnp.where(first, v, -v)

    for ch in range(2):
        arrive(recv_ab.at[ch], in_sem1.at[ch])
        x = recv_ab.at[ch].reshape(FINE, 128)[...]
        v = 0.0
        for half in range(2):
            v += transform(
                2 * ch + half, x, lambda p: p,
                lambda lane, wave: lane // 32 == 2 * half + wave,
            )
        back_ab.at[ch].reshape(COARSE, 128)[...] = hemispheres(v).astype(BF)
        exchange(back_ab.at[ch], home_ab.at[ch], out_sem2.at[ch], in_sem2.at[ch])

    arrive(recv_c, in_sem1.at[2])
    x = recv_c.reshape(FINE // 2, 128)[...].astype(F32)
    upper = (lanes(x.shape) // 32) % 2 == 0
    wide[pl.ds(0, FINE // 2, stride=2), :] = jnp.where(upper, x, 0.0)
    wide[pl.ds(1, FINE // 2, stride=2), :] = jnp.where(upper, 0.0, x)
    v = transform(
        4, wide[...].astype(BF), lambda p: p + pltpu.roll(p, 96, 1),
        lambda lane, wave: lane // 32 == 2 * wave,
    )
    wide[:COARSE] = hemispheres(v)
    for k in range(CBAND // 2):
        a = wide[pl.ds(2 * k, BANDS, stride=CBAND), :]
        b = wide[pl.ds(2 * k + 1, BANDS, stride=CBAND), :]
        narrow[pl.ds(k, BANDS, stride=6), :] = jnp.where(
            (lanes(a.shape) // 32) % 2 == 0, a, pltpu.roll(b, 32, 1)
        )
    narrow[pl.ds(5, BANDS, stride=6), :] = jnp.zeros((BANDS, 128), F32)
    back_c.reshape(6 * BANDS, 128)[...] = narrow[...].astype(BF)
    exchange(back_c, home_c, out_sem2.at[2], in_sem2.at[2])

    def place(first, columns):
        count = columns.shape[0]
        return lax.dot_general(
            columns, sel[first : first + count, :], (((0,), (0,)), ((), ())),
            preferred_element_type=F32,
        )

    for ch in range(2):
        arrive(home_ab.at[ch], in_sem2.at[ch])
        wide[:COARSE] = home_ab.at[ch].reshape(COARSE, 128)[...].astype(F32)
        groups = []
        for q in range(3):
            js = [min(4 * q + k, CBAND - 1) for k in range(4)]
            groups.append(
                jnp.concatenate(
                    block_transpose([wide[pl.ds(j, BANDS, stride=CBAND), :] for j in js]), axis=0
                ).astype(BF)
            )
        placed = place(256 * ch, jnp.concatenate(groups, axis=1))
        if ch == 0:
            acc[...] = placed
        else:
            acc[...] += placed
    arrive(home_c, in_sem2.at[2])
    wide[: 6 * BANDS] = home_c.reshape(6 * BANDS, 128)[...].astype(F32)
    groups = []
    for q in range(3):
        parts = half_swap(*[wide[pl.ds(2 * q + k, BANDS, stride=6), :] for k in range(2)])
        groups.append(jnp.concatenate(parts, axis=0).astype(BF))
    placed = place(512, jnp.concatenate(groups, axis=1))
    for j in range(CBAND):
        rows = acc[32 * j : 32 * (j + 1), :] + placed[32 * j : 32 * (j + 1)]
        kept = 2 * lanes(rows.shape) < 20 + 4 * (me * CBAND + j)
        rows = jnp.where(kept, rows, 0.0).astype(BF)
        for h in range(2):
            for c in range(2):
                at = 16 * h + 8 * c
                out_ref[h, j, :, c * WAVES : (c + 1) * WAVES] = rows[at : at + 8]

    for ch in range(2):
        left(send_ab.at[ch], out_sem1.at[ch])
        left(back_ab.at[ch], out_sem2.at[ch])
    left(send_c, out_sem1.at[2])
    left(back_c, out_sem2.at[2])


def on_device(fine_field, fwd_table, inv_table, pair_order):
    vmem = pl.BlockSpec(memory_space=pltpu.VMEM)
    hbm = pl.BlockSpec(memory_space=pltpu.HBM)
    ab1 = (2, BANDS, BAND // 2, 2, 128)
    c1 = (BANDS, BAND // 4, 2, 128)
    ab2 = (2, BANDS, CBAND // 2, 2, 128)
    c2 = (BANDS, 3, 2, 128)
    return pl.pallas_call(
        kernel,
        out_shape=jax.ShapeDtypeStruct((2, CBAND, 8, 2 * WAVES), BF),
        in_specs=[hbm] * 4,
        out_specs=vmem,
        scratch_shapes=[
            pltpu.SMEM((PAIRS,), jnp.int32),
            pltpu.VMEM((PAIRS,), jnp.int32),
            pltpu.VMEM((PAIRS, 128), jnp.int32),
            pltpu.VMEM((2, BAND, 8, 2 * WAVES), BF),
            pltpu.VMEM((SLOTS, ROWS, FINE), BF),
            pltpu.VMEM((SLOTS, ROWS, COARSE), BF),
            pltpu.VMEM((BAND * 32, WAVES), BF),
            pltpu.VMEM((WAVES, WAVES), BF),
            pltpu.VMEM((WAVES, WAVES), BF),
            pltpu.VMEM((FINE, 128), F32),
            pltpu.VMEM((6 * BANDS, 128), F32),
            pltpu.VMEM((384, WAVES), F32),
            pltpu.VMEM(ab1, BF), pltpu.VMEM(c1, BF),
            pltpu.VMEM(ab1, BF), pltpu.VMEM(c1, BF),
            pltpu.VMEM(ab2, BF), pltpu.VMEM(c2, BF),
            pltpu.VMEM(ab2, BF), pltpu.VMEM(c2, BF),
            pltpu.SemaphoreType.DMA((2,)), pltpu.SemaphoreType.DMA((BAND // 4,)),
            pltpu.SemaphoreType.DMA((SLOTS,)), pltpu.SemaphoreType.DMA((SLOTS,)),
            pltpu.SemaphoreType.DMA((3,)), pltpu.SemaphoreType.DMA((3,)),
            pltpu.SemaphoreType.DMA((3,)), pltpu.SemaphoreType.DMA((3,)),
        ],
        compiler_params=pltpu.CompilerParams(
            collective_id=0, has_side_effects=True, vmem_limit_bytes=55500000
        ),
    )(pair_order, fine_field, fwd_table, inv_table)


def solution(mesh):
    return jax.shard_map(
        on_device,
        mesh=mesh,
        in_specs=(P(None, "lat", "lev", None), P("lat", None, None), P("lat", None, None), P()),
        out_specs=P(None, "lat", "lev", None),
        check_vma=False,
    )
```

```python
import jax
import jax.numpy as jnp
from jax import lax
from jax.experimental import pallas as pl
from jax.experimental.pallas import tpu as pltpu
from jax.sharding import PartitionSpec as P

MESH = pl.DeviceIdType.MESH
WAVES = 640
FINE = 1280
COARSE = 640
BANDS = 64
BAND = FINE // BANDS
CBAND = COARSE // BANDS
SLOTS = 5
PAIRS = BANDS * SLOTS
ROWS = 641
ORDER = [
    x * 16 + z * 2 + core
    for core in (1, 0)
    for x in (2, 1, 3, 0)
    for z in (4, 3, 5, 2, 6, 1, 7, 0)
    if (x, z, core) != (0, 0, 0)
]
BF = jnp.bfloat16
F32 = jnp.float32


def lanes(shape):
    return lax.broadcasted_iota(jnp.int32, shape, len(shape) - 1)


def block_transpose(a):
    lane = lanes(a[0].shape)
    low = lane < 64
    even = (lane // 32) % 2 == 0
    c0 = jnp.where(low, a[0], pltpu.roll(a[2], 64, 1))
    c2 = jnp.where(low, pltpu.roll(a[0], 64, 1), a[2])
    c1 = jnp.where(low, a[1], pltpu.roll(a[3], 64, 1))
    c3 = jnp.where(low, pltpu.roll(a[1], 64, 1), a[3])
    b0 = jnp.where(even, c0, pltpu.roll(c1, 32, 1))
    b1 = jnp.where(even, pltpu.roll(c0, 96, 1), c1)
    b2 = jnp.where(even, c2, pltpu.roll(c3, 32, 1))
    b3 = jnp.where(even, pltpu.roll(c2, 96, 1), c3)
    return b0, b1, b2, b3


def half_swap(a, b):
    low = lanes(a.shape) < 64
    return (
        jnp.where(low, a, pltpu.roll(b, 64, 1)),
        jnp.where(low, pltpu.roll(a, 64, 1), b),
    )


def kernel(
    pair_hbm, fine_hbm, fwd_hbm, inv_hbm, out_ref,
    pair_ref, line, column, fine_ref, fwd, inv, folded, sel, turned, wide, narrow, acc,
    send_ab, send_c, recv_ab, recv_c, back_ab, back_c, home_ab, home_c,
    pair_sem, fine_sem, fwd_sem, inv_sem, out_sem1, in_sem1, out_sem2, in_sem2,
):
    me = lax.axis_index("lat")
    lev = lax.axis_index("lev")
    barrier = pltpu.get_barrier_semaphore()

    pieces = BAND // 4
    pair_copies = [
        pltpu.make_async_copy(pair_hbm, line, pair_sem.at[0]),
        pltpu.make_async_copy(pair_hbm, pair_ref, pair_sem.at[1]),
    ]
    fine_copies = [
        pltpu.make_async_copy(
            fine_hbm.at[:, pl.ds(4 * q, 4)], fine_ref.at[:, pl.ds(4 * q, 4)], fine_sem.at[q]
        )
        for q in range(pieces)
    ]
    for copy in pair_copies + fine_copies:
        copy.start()

    @pl.loop(1, BANDS, unroll=True)
    def _(t):
        pl.semaphore_signal(
            barrier, inc=1, device_id=(lax.rem(me + t, BANDS), lev), device_id_type=MESH
        )


    pair_copies[0].wait()
    column[...] = jnp.transpose(jnp.broadcast_to(line[...].reshape(1, PAIRS), (128, PAIRS)))
    for slot in range(SLOTS):
        low = column[pl.ds(slot, BANDS, stride=SLOTS), :]
        for k, wave in enumerate((low, WAVES - 1 - low)):
            at = (2 * slot + k) * BANDS
            for b in range(WAVES // 128):
                sel[at : at + BANDS, 128 * b : 128 * (b + 1)] = jnp.where(
                    wave == lanes(wave.shape) + 128 * b, 1.0, 0.0
                ).astype(BF)

    for at in (0, 256, 512):
        count = min(256, WAVES - at)
        turned[:, at : at + count] = jnp.transpose(sel[at : at + count, :])

    def fold(i):
        north = fine_ref[0, i].astype(F32)
        south = fine_ref[1, i].astype(F32)
        m = lanes((8, 2 * WAVES))
        m = jnp.where(m >= WAVES, m - WAVES, m)
        kept = 2 * m < 20 + 4 * (me * BAND + i)
        even = jnp.where(kept, north + south, 0.0)
        odd = jnp.where(kept, north - south, 0.0)
        rows = jnp.concatenate(
            [even[:, :WAVES], even[:, WAVES:], odd[:, :WAVES], odd[:, WAVES:]], axis=0
        )
        folded[32 * i : 32 * (i + 1), :] = rows.astype(BF)

    def facing(a, b, high):
        low = lanes(a.shape) < 64
        if high:
            return jnp.where(low, pltpu.roll(a, 64, 1), b)
        return jnp.where(low, a, pltpu.roll(b, 64, 1))

    def pick(first, count):
        g = jnp.dot(
            folded[...], turned[:, first : first + count], preferred_element_type=F32
        )
        return [g[32 * i : 32 * (i + 1)] for i in range(BAND)]

    def exchange(src, dst, out_sem, in_sem):
        pltpu.make_async_copy(src.at[me], dst.at[me], in_sem).start()

        for t in ORDER:
            to = lax.rem(me + t, BANDS)
            pltpu.make_async_remote_copy(
                src_ref=src.at[to], dst_ref=dst.at[me], send_sem=out_sem, recv_sem=in_sem,
                device_id=(to, lev), device_id_type=MESH,
            ).start()

    def arrive(dst, in_sem):
        pltpu.make_async_copy(dst, dst, in_sem).wait()

    def left(src, out_sem):
        part = src.at[pl.ds(0, BANDS - 1)]
        pltpu.make_async_copy(part, part, out_sem).wait()

    for q in range(pieces):
        fine_copies[q].wait()
        for i in range(4 * q, 4 * (q + 1)):
            fold(i)
    for ch in range(2):
        g = pick(256 * ch, 256)
        for i in range(0, BAND, 2):
            blocks = []
            for k in range(4):
                at = 128 * (k // 2)
                a, b = g[i][:, at : at + 128], g[i + 1][:, at : at + 128]
                blocks.append(facing(a, b, k % 2 == 1))
            rows = jnp.transpose(jnp.concatenate(blocks, axis=0))
            for k in range(2):
                wide[pl.ds(i + k, BANDS, stride=BAND), :] = rows[64 * k : 64 * (k + 1)]
        send_ab.at[ch].reshape(FINE, 128)[...] = wide[...].astype(BF)
        if ch == 0:
            pl.semaphore_wait(barrier, BANDS - 1)
        exchange(send_ab.at[ch], recv_ab.at[ch], out_sem1.at[ch], in_sem1.at[ch])

    g = pick(512, 128)
    for i in range(0, BAND, 4):
        blocks = [facing(g[i + k % 2], g[i + 2 + k % 2], k >= 2) for k in range(4)]
        rows = jnp.transpose(jnp.concatenate(blocks, axis=0))
        for k in range(2):
            wide[pl.ds(i // 2 + k, BANDS, stride=BAND // 2), :] = rows[64 * k : 64 * (k + 1)]
    send_c.reshape(FINE // 2, 128)[...] = wide[: FINE // 2].astype(BF)
    exchange(send_c, recv_c, out_sem1.at[2], in_sem1.at[2])
    for s in range(SLOTS):
        pltpu.make_async_copy(fwd_hbm.at[s], fwd.at[s], fwd_sem.at[s]).start()
        pltpu.make_async_copy(inv_hbm.at[s], inv.at[s], inv_sem.at[s]).start()

    pair_copies[1].wait()
    row = lax.broadcasted_iota(jnp.int32, (ROWS, 128), 0)
    lane = lanes((ROWS, 128))

    def transform(slot, x, fold_lanes, owned):
        pltpu.make_async_copy(fwd_hbm.at[slot], fwd.at[slot], fwd_sem.at[slot]).wait()
        product = jnp.dot(fwd[slot], x, preferred_element_type=F32)
        product = fold_lanes(product)
        boundary = WAVES - pair_ref[me * SLOTS + slot]
        second = row >= boundary
        parity = jnp.where(second, row - boundary, row) % 2
        wave = second.astype(jnp.int32)
        keep = owned(lane, wave) & ((lane // 16) % 2 == parity)
        spectra = jnp.where(keep, product, 0.0).astype(BF)
        pltpu.make_async_copy(inv_hbm.at[slot], inv.at[slot], inv_sem.at[slot]).wait()
        return lax.dot_general(
            inv[slot], spectra, (((0,), (0,)), ((), ())), preferred_element_type=F32
        )

    def hemispheres(v):
        first = (lanes(v.shape) // 16) % 2 == 0
        other = jnp.where(first, pltpu.roll(v, 112, 1), pltpu.roll(v, 16, 1))
        return other + jnp.where(first, v, -v)

    for ch in range(2):
        arrive(recv_ab.at[ch], in_sem1.at[ch])
        x = recv_ab.at[ch].reshape(FINE, 128)[...]
        v = 0.0
        for half in range(2):
            v += transform(
                2 * ch + half, x, lambda p: p,
                lambda lane, wave: lane // 32 == 2 * half + wave,
            )
        back_ab.at[ch].reshape(COARSE, 128)[...] = hemispheres(v).astype(BF)
        exchange(back_ab.at[ch], home_ab.at[ch], out_sem2.at[ch], in_sem2.at[ch])

    arrive(recv_c, in_sem1.at[2])
    x = recv_c.reshape(FINE // 2, 128)[...].astype(F32)
    upper = (lanes(x.shape) // 32) % 2 == 0
    wide[pl.ds(0, FINE // 2, stride=2), :] = jnp.where(upper, x, 0.0)
    wide[pl.ds(1, FINE // 2, stride=2), :] = jnp.where(upper, 0.0, x)
    v = transform(
        4, wide[...].astype(BF), lambda p: p + pltpu.roll(p, 96, 1),
        lambda lane, wave: lane // 32 == 2 * wave,
    )
    wide[:COARSE] = hemispheres(v)
    for k in range(CBAND // 2):
        a = wide[pl.ds(2 * k, BANDS, stride=CBAND), :]
        b = wide[pl.ds(2 * k + 1, BANDS, stride=CBAND), :]
        narrow[pl.ds(k, BANDS, stride=6), :] = jnp.where(
            (lanes(a.shape) // 32) % 2 == 0, a, pltpu.roll(b, 32, 1)
        )
    narrow[pl.ds(5, BANDS, stride=6), :] = jnp.zeros((BANDS, 128), F32)
    back_c.reshape(6 * BANDS, 128)[...] = narrow[...].astype(BF)
    exchange(back_c, home_c, out_sem2.at[2], in_sem2.at[2])

    def place(first, columns):
        count = columns.shape[0]
        return lax.dot_general(
            columns, sel[first : first + count, :], (((0,), (0,)), ((), ())),
            preferred_element_type=F32,
        )

    for ch in range(2):
        arrive(home_ab.at[ch], in_sem2.at[ch])
        wide[:COARSE] = home_ab.at[ch].reshape(COARSE, 128)[...].astype(F32)
        groups = []
        for q in range(3):
            js = [min(4 * q + k, CBAND - 1) for k in range(4)]
            groups.append(
                jnp.concatenate(
                    block_transpose([wide[pl.ds(j, BANDS, stride=CBAND), :] for j in js]), axis=0
                ).astype(BF)
            )
        placed = place(256 * ch, jnp.concatenate(groups, axis=1)[:, :320])
        if ch == 0:
            acc[...] = placed
        else:
            acc[...] += placed
    arrive(home_c, in_sem2.at[2])
    wide[: 6 * BANDS] = home_c.reshape(6 * BANDS, 128)[...].astype(F32)
    groups = []
    for q in range(3):
        parts = half_swap(*[wide[pl.ds(2 * q + k, BANDS, stride=6), :] for k in range(2)])
        groups.append(jnp.concatenate(parts, axis=0).astype(BF))
    placed = place(512, jnp.concatenate(groups, axis=1)[:, :320])
    for j in range(CBAND):
        rows = acc[32 * j : 32 * (j + 1), :] + placed[32 * j : 32 * (j + 1)]
        kept = 2 * lanes(rows.shape) < 20 + 4 * (me * CBAND + j)
        rows = jnp.where(kept, rows, 0.0).astype(BF)
        for h in range(2):
            for c in range(2):
                at = 16 * h + 8 * c
                out_ref[h, j, :, c * WAVES : (c + 1) * WAVES] = rows[at : at + 8]

    for ch in range(2):
        left(send_ab.at[ch], out_sem1.at[ch])
        left(back_ab.at[ch], out_sem2.at[ch])
    left(send_c, out_sem1.at[2])
    left(back_c, out_sem2.at[2])


def on_device(fine_field, fwd_table, inv_table, pair_order):
    vmem = pl.BlockSpec(memory_space=pltpu.VMEM)
    hbm = pl.BlockSpec(memory_space=pltpu.HBM)
    ab1 = (2, BANDS, BAND // 2, 2, 128)
    c1 = (BANDS, BAND // 4, 2, 128)
    ab2 = (2, BANDS, CBAND // 2, 2, 128)
    c2 = (BANDS, 3, 2, 128)
    return pl.pallas_call(
        kernel,
        out_shape=jax.ShapeDtypeStruct((2, CBAND, 8, 2 * WAVES), BF),
        in_specs=[hbm] * 4,
        out_specs=vmem,
        scratch_shapes=[
            pltpu.SMEM((PAIRS,), jnp.int32),
            pltpu.VMEM((PAIRS,), jnp.int32),
            pltpu.VMEM((PAIRS, 128), jnp.int32),
            pltpu.VMEM((2, BAND, 8, 2 * WAVES), BF),
            pltpu.VMEM((SLOTS, ROWS, FINE), BF),
            pltpu.VMEM((SLOTS, ROWS, COARSE), BF),
            pltpu.VMEM((BAND * 32, WAVES), BF),
            pltpu.VMEM((WAVES, WAVES), BF),
            pltpu.VMEM((WAVES, WAVES), BF),
            pltpu.VMEM((FINE, 128), F32),
            pltpu.VMEM((6 * BANDS, 128), F32),
            pltpu.VMEM((320, WAVES), F32),
            pltpu.VMEM(ab1, BF), pltpu.VMEM(c1, BF),
            pltpu.VMEM(ab1, BF), pltpu.VMEM(c1, BF),
            pltpu.VMEM(ab2, BF), pltpu.VMEM(c2, BF),
            pltpu.VMEM(ab2, BF), pltpu.VMEM(c2, BF),
            pltpu.SemaphoreType.DMA((2,)), pltpu.SemaphoreType.DMA((BAND // 4,)),
            pltpu.SemaphoreType.DMA((SLOTS,)), pltpu.SemaphoreType.DMA((SLOTS,)),
            pltpu.SemaphoreType.DMA((3,)), pltpu.SemaphoreType.DMA((3,)),
            pltpu.SemaphoreType.DMA((3,)), pltpu.SemaphoreType.DMA((3,)),
        ],
        compiler_params=pltpu.CompilerParams(
            collective_id=0, has_side_effects=True, vmem_limit_bytes=55500000
        ),
    )(pair_order, fine_field, fwd_table, inv_table)


def solution(mesh):
    return jax.shard_map(
        on_device,
        mesh=mesh,
        in_specs=(P(None, "lat", "lev", None), P("lat", None, None), P("lat", None, None), P()),
        out_specs=P(None, "lat", "lev", None),
        check_vma=False,
    )
```

```python
import jax
import jax.numpy as jnp
from jax import lax
from jax.experimental import pallas as pl
from jax.experimental.pallas import tpu as pltpu
from jax.sharding import PartitionSpec as P

MESH = pl.DeviceIdType.MESH
WAVES = 640
FINE = 1280
COARSE = 640
BANDS = 64
BAND = FINE // BANDS
CBAND = COARSE // BANDS
SLOTS = 5
PAIRS = BANDS * SLOTS
ROWS = 641
ORDER = [
    x * 16 + z * 2 + core
    for core in (1, 0)
    for x in (2, 1, 3, 0)
    for z in (4, 3, 5, 2, 6, 1, 7, 0)
    if (x, z, core) != (0, 0, 0)
]
BF = jnp.bfloat16
F32 = jnp.float32


def lanes(shape):
    return lax.broadcasted_iota(jnp.int32, shape, len(shape) - 1)


def block_transpose(a):
    lane = lanes(a[0].shape)
    low = lane < 64
    even = (lane // 32) % 2 == 0
    c0 = jnp.where(low, a[0], pltpu.roll(a[2], 64, 1))
    c2 = jnp.where(low, pltpu.roll(a[0], 64, 1), a[2])
    c1 = jnp.where(low, a[1], pltpu.roll(a[3], 64, 1))
    c3 = jnp.where(low, pltpu.roll(a[1], 64, 1), a[3])
    b0 = jnp.where(even, c0, pltpu.roll(c1, 32, 1))
    b1 = jnp.where(even, pltpu.roll(c0, 96, 1), c1)
    b2 = jnp.where(even, c2, pltpu.roll(c3, 32, 1))
    b3 = jnp.where(even, pltpu.roll(c2, 96, 1), c3)
    return b0, b1, b2, b3


def half_swap(a, b):
    low = lanes(a.shape) < 64
    return (
        jnp.where(low, a, pltpu.roll(b, 64, 1)),
        jnp.where(low, pltpu.roll(a, 64, 1), b),
    )


def kernel(
    pair_hbm, fine_hbm, fwd_hbm, inv_hbm, out_ref,
    pair_ref, line, column, fine_ref, fwd, inv, folded, sel, turned, wide, narrow, acc,
    send_ab, send_c, recv_ab, recv_c, back_ab, back_c, home_ab, home_c,
    pair_sem, fine_sem, fwd_sem, inv_sem, out_sem1, in_sem1, out_sem2, in_sem2,
):
    me = lax.axis_index("lat")
    lev = lax.axis_index("lev")
    barrier = pltpu.get_barrier_semaphore()

    pieces = BAND // 4
    pair_copies = [
        pltpu.make_async_copy(pair_hbm, line, pair_sem.at[0]),
        pltpu.make_async_copy(pair_hbm, pair_ref, pair_sem.at[1]),
    ]
    fine_copies = [
        pltpu.make_async_copy(
            fine_hbm.at[:, pl.ds(4 * q, 4)], fine_ref.at[:, pl.ds(4 * q, 4)], fine_sem.at[q]
        )
        for q in range(pieces)
    ]
    for copy in pair_copies + fine_copies:
        copy.start()

    for t in ORDER:
        pl.semaphore_signal(
            barrier, inc=1, device_id=(lax.rem(me + t, BANDS), lev), device_id_type=MESH
        )


    pair_copies[0].wait()
    column[...] = jnp.transpose(jnp.broadcast_to(line[...].reshape(1, PAIRS), (128, PAIRS)))
    for slot in range(SLOTS):
        low = column[pl.ds(slot, BANDS, stride=SLOTS), :]
        for k, wave in enumerate((low, WAVES - 1 - low)):
            at = (2 * slot + k) * BANDS
            for b in range(WAVES // 128):
                sel[at : at + BANDS, 128 * b : 128 * (b + 1)] = jnp.where(
                    wave == lanes(wave.shape) + 128 * b, 1.0, 0.0
                ).astype(BF)

    for at in (0, 256, 512):
        count = min(256, WAVES - at)
        turned[:, at : at + count] = jnp.transpose(sel[at : at + count, :])

    def fold(i):
        north = fine_ref[0, i].astype(F32)
        south = fine_ref[1, i].astype(F32)
        m = lanes((8, 2 * WAVES))
        m = jnp.where(m >= WAVES, m - WAVES, m)
        kept = 2 * m < 20 + 4 * (me * BAND + i)
        even = jnp.where(kept, north + south, 0.0)
        odd = jnp.where(kept, north - south, 0.0)
        rows = jnp.concatenate(
            [even[:, :WAVES], even[:, WAVES:], odd[:, :WAVES], odd[:, WAVES:]], axis=0
        )
        folded[32 * i : 32 * (i + 1), :] = rows.astype(BF)

    def facing(a, b, high):
        low = lanes(a.shape) < 64
        if high:
            return jnp.where(low, pltpu.roll(a, 64, 1), b)
        return jnp.where(low, a, pltpu.roll(b, 64, 1))

    def pick(first, count):
        g = jnp.dot(
            folded[...], turned[:, first : first + count], preferred_element_type=F32
        )
        return [g[32 * i : 32 * (i + 1)] for i in range(BAND)]

    def exchange(src, dst, out_sem, in_sem):
        pltpu.make_async_copy(src.at[me], dst.at[me], in_sem).start()

        for t in ORDER:
            to = lax.rem(me + t, BANDS)
            pltpu.make_async_remote_copy(
                src_ref=src.at[to], dst_ref=dst.at[me], send_sem=out_sem, recv_sem=in_sem,
                device_id=(to, lev), device_id_type=MESH,
            ).start()

    def arrive(dst, in_sem):
        pltpu.make_async_copy(dst, dst, in_sem).wait()

    def left(src, out_sem):
        part = src.at[pl.ds(0, BANDS - 1)]
        pltpu.make_async_copy(part, part, out_sem).wait()

    for q in range(pieces):
        fine_copies[q].wait()
        for i in range(4 * q, 4 * (q + 1)):
            fold(i)
    for ch in range(2):
        g = pick(256 * ch, 256)
        for i in range(0, BAND, 2):
            blocks = []
            for k in range(4):
                at = 128 * (k // 2)
                a, b = g[i][:, at : at + 128], g[i + 1][:, at : at + 128]
                blocks.append(facing(a, b, k % 2 == 1))
            rows = jnp.transpose(jnp.concatenate(blocks, axis=0))
            for k in range(2):
                wide[pl.ds(i + k, BANDS, stride=BAND), :] = rows[64 * k : 64 * (k + 1)]
        send_ab.at[ch].reshape(FINE, 128)[...] = wide[...].astype(BF)
        if ch == 0:
            pl.semaphore_wait(barrier, BANDS - 1)
        exchange(send_ab.at[ch], recv_ab.at[ch], out_sem1.at[ch], in_sem1.at[ch])

    g = pick(512, 128)
    for i in range(0, BAND, 4):
        blocks = [facing(g[i + k % 2], g[i + 2 + k % 2], k >= 2) for k in range(4)]
        rows = jnp.transpose(jnp.concatenate(blocks, axis=0))
        for k in range(2):
            wide[pl.ds(i // 2 + k, BANDS, stride=BAND // 2), :] = rows[64 * k : 64 * (k + 1)]
    send_c.reshape(FINE // 2, 128)[...] = wide[: FINE // 2].astype(BF)
    exchange(send_c, recv_c, out_sem1.at[2], in_sem1.at[2])
    for s in range(SLOTS):
        pltpu.make_async_copy(fwd_hbm.at[s], fwd.at[s], fwd_sem.at[s]).start()
        pltpu.make_async_copy(inv_hbm.at[s], inv.at[s], inv_sem.at[s]).start()

    pair_copies[1].wait()
    row = lax.broadcasted_iota(jnp.int32, (ROWS, 128), 0)
    lane = lanes((ROWS, 128))

    def transform(slot, x, fold_lanes, owned):
        pltpu.make_async_copy(fwd_hbm.at[slot], fwd.at[slot], fwd_sem.at[slot]).wait()
        product = jnp.dot(fwd[slot], x, preferred_element_type=F32)
        product = fold_lanes(product)
        boundary = WAVES - pair_ref[me * SLOTS + slot]
        second = row >= boundary
        parity = jnp.where(second, row - boundary, row) % 2
        wave = second.astype(jnp.int32)
        keep = owned(lane, wave) & ((lane // 16) % 2 == parity)
        spectra = jnp.where(keep, product, 0.0).astype(BF)
        pltpu.make_async_copy(inv_hbm.at[slot], inv.at[slot], inv_sem.at[slot]).wait()
        return lax.dot_general(
            inv[slot], spectra, (((0,), (0,)), ((), ())), preferred_element_type=F32
        )

    def hemispheres(v):
        first = (lanes(v.shape) // 16) % 2 == 0
        other = jnp.where(first, pltpu.roll(v, 112, 1), pltpu.roll(v, 16, 1))
        return other + jnp.where(first, v, -v)

    for ch in range(2):
        arrive(recv_ab.at[ch], in_sem1.at[ch])
        x = recv_ab.at[ch].reshape(FINE, 128)[...]
        v = 0.0
        for half in range(2):
            v += transform(
                2 * ch + half, x, lambda p: p,
                lambda lane, wave: lane // 32 == 2 * half + wave,
            )
        back_ab.at[ch].reshape(COARSE, 128)[...] = hemispheres(v).astype(BF)
        exchange(back_ab.at[ch], home_ab.at[ch], out_sem2.at[ch], in_sem2.at[ch])

    arrive(recv_c, in_sem1.at[2])
    x = recv_c.reshape(FINE // 2, 128)[...].astype(F32)
    upper = (lanes(x.shape) // 32) % 2 == 0
    wide[pl.ds(0, FINE // 2, stride=2), :] = jnp.where(upper, x, 0.0)
    wide[pl.ds(1, FINE // 2, stride=2), :] = jnp.where(upper, 0.0, x)
    v = transform(
        4, wide[...].astype(BF), lambda p: p + pltpu.roll(p, 96, 1),
        lambda lane, wave: lane // 32 == 2 * wave,
    )
    wide[:COARSE] = hemispheres(v)
    for k in range(CBAND // 2):
        a = wide[pl.ds(2 * k, BANDS, stride=CBAND), :]
        b = wide[pl.ds(2 * k + 1, BANDS, stride=CBAND), :]
        narrow[pl.ds(k, BANDS, stride=6), :] = jnp.where(
            (lanes(a.shape) // 32) % 2 == 0, a, pltpu.roll(b, 32, 1)
        )
    narrow[pl.ds(5, BANDS, stride=6), :] = jnp.zeros((BANDS, 128), F32)
    back_c.reshape(6 * BANDS, 128)[...] = narrow[...].astype(BF)
    exchange(back_c, home_c, out_sem2.at[2], in_sem2.at[2])

    def place(first, columns):
        count = columns.shape[0]
        return lax.dot_general(
            columns, sel[first : first + count, :], (((0,), (0,)), ((), ())),
            preferred_element_type=F32,
        )

    for ch in range(2):
        arrive(home_ab.at[ch], in_sem2.at[ch])
        wide[:COARSE] = home_ab.at[ch].reshape(COARSE, 128)[...].astype(F32)
        groups = []
        for q in range(3):
            js = [min(4 * q + k, CBAND - 1) for k in range(4)]
            groups.append(
                jnp.concatenate(
                    block_transpose([wide[pl.ds(j, BANDS, stride=CBAND), :] for j in js]), axis=0
                ).astype(BF)
            )
        placed = place(256 * ch, jnp.concatenate(groups, axis=1)[:, :320])
        if ch == 0:
            acc[...] = placed
        else:
            acc[...] += placed
    arrive(home_c, in_sem2.at[2])
    wide[: 6 * BANDS] = home_c.reshape(6 * BANDS, 128)[...].astype(F32)
    groups = []
    for q in range(3):
        parts = half_swap(*[wide[pl.ds(2 * q + k, BANDS, stride=6), :] for k in range(2)])
        groups.append(jnp.concatenate(parts, axis=0).astype(BF))
    placed = place(512, jnp.concatenate(groups, axis=1)[:, :320])
    for j in range(CBAND):
        rows = acc[32 * j : 32 * (j + 1), :] + placed[32 * j : 32 * (j + 1)]
        kept = 2 * lanes(rows.shape) < 20 + 4 * (me * CBAND + j)
        rows = jnp.where(kept, rows, 0.0).astype(BF)
        for h in range(2):
            for c in range(2):
                at = 16 * h + 8 * c
                out_ref[h, j, :, c * WAVES : (c + 1) * WAVES] = rows[at : at + 8]

    for ch in range(2):
        left(send_ab.at[ch], out_sem1.at[ch])
        left(back_ab.at[ch], out_sem2.at[ch])
    left(send_c, out_sem1.at[2])
    left(back_c, out_sem2.at[2])


def on_device(fine_field, fwd_table, inv_table, pair_order):
    vmem = pl.BlockSpec(memory_space=pltpu.VMEM)
    hbm = pl.BlockSpec(memory_space=pltpu.HBM)
    ab1 = (2, BANDS, BAND // 2, 2, 128)
    c1 = (BANDS, BAND // 4, 2, 128)
    ab2 = (2, BANDS, CBAND // 2, 2, 128)
    c2 = (BANDS, 3, 2, 128)
    return pl.pallas_call(
        kernel,
        out_shape=jax.ShapeDtypeStruct((2, CBAND, 8, 2 * WAVES), BF),
        in_specs=[hbm] * 4,
        out_specs=vmem,
        scratch_shapes=[
            pltpu.SMEM((PAIRS,), jnp.int32),
            pltpu.VMEM((PAIRS,), jnp.int32),
            pltpu.VMEM((PAIRS, 128), jnp.int32),
            pltpu.VMEM((2, BAND, 8, 2 * WAVES), BF),
            pltpu.VMEM((SLOTS, ROWS, FINE), BF),
            pltpu.VMEM((SLOTS, ROWS, COARSE), BF),
            pltpu.VMEM((BAND * 32, WAVES), BF),
            pltpu.VMEM((WAVES, WAVES), BF),
            pltpu.VMEM((WAVES, WAVES), BF),
            pltpu.VMEM((FINE, 128), F32),
            pltpu.VMEM((6 * BANDS, 128), F32),
            pltpu.VMEM((320, WAVES), F32),
            pltpu.VMEM(ab1, BF), pltpu.VMEM(c1, BF),
            pltpu.VMEM(ab1, BF), pltpu.VMEM(c1, BF),
            pltpu.VMEM(ab2, BF), pltpu.VMEM(c2, BF),
            pltpu.VMEM(ab2, BF), pltpu.VMEM(c2, BF),
            pltpu.SemaphoreType.DMA((2,)), pltpu.SemaphoreType.DMA((BAND // 4,)),
            pltpu.SemaphoreType.DMA((SLOTS,)), pltpu.SemaphoreType.DMA((SLOTS,)),
            pltpu.SemaphoreType.DMA((3,)), pltpu.SemaphoreType.DMA((3,)),
            pltpu.SemaphoreType.DMA((3,)), pltpu.SemaphoreType.DMA((3,)),
        ],
        compiler_params=pltpu.CompilerParams(
            collective_id=0, has_side_effects=True, vmem_limit_bytes=55500000
        ),
    )(pair_order, fine_field, fwd_table, inv_table)


def solution(mesh):
    return jax.shard_map(
        on_device,
        mesh=mesh,
        in_specs=(P(None, "lat", "lev", None), P("lat", None, None), P("lat", None, None), P()),
        out_specs=P(None, "lat", "lev", None),
        check_vma=False,
    )
```
